256 devices in a mesh: dp: 8 (over x, core), tensor: 32 (over z, y).
Axes of the slice: x: 4, y: 4, z: 8, core: 2. Of those that a mesh axis runs over, the one named last changes fastest.
Arguments:
- acts: bfloat16 [3072, 8192], P('dp', 'tensor'), may hold values from -6 to 6
- gate_weight: bfloat16 [8192, 16384], P(None, 'tensor'), may hold values from -0.0625 to 0.0625
Outputs:
- covariance: float32 [8192, 8192], P('tensor', 'dp')
- gate_out: bfloat16 [3072, 16384], P('dp', 'tensor')
The draws below stay inside these ranges and needn't reach their ends.
All inputs are finite; a program needn't handle non-finite values.
Results may differ from the reference program's by a relative error of at most 0.001.
Values may be sent and summed in bfloat16 or wider, within the bound.
A program may use at most 64 MiB of HBM per device.

```python
import jax
import jax.numpy as jnp

D = 8192
FF = 16384
TOKENS = 3072


def block_levels(own_key, shape, shards, least, top_value):
    loudness, own = 1.0, jax.random.fold_in(own_key, 6)
    for dim, blocks in shards:
        draws = jnp.exp(jax.random.uniform(jax.random.fold_in(own, dim), (blocks,), jnp.float32, least / len(shards), top_value / len(shards)))
        loudness = loudness * jnp.repeat(draws, shape[dim] // blocks).reshape([-1 if axis == dim else 1 for axis in range(len(shape))])
    return loudness


def bell_draw(key, dims, scale, reach, cuts=(), dtype=jnp.bfloat16):
    result = scale * jax.random.normal(key, dims, jnp.float32)
    if cuts:
        result = result * block_levels(key, dims, cuts, -0.22, 0.18)
    return jnp.clip(result, -reach, reach).astype(dtype)


def setup_inputs(seed: int = 0) -> dict:
    key_of = jax.random.split(jax.random.key(seed), 3)
    return {
        "acts": bell_draw(key_of[0], (TOKENS, D), 1.0, 6.0, ((0, 8), (1, 32))),
        "gate_weight": bell_draw(key_of[1], (D, FF), D ** -0.5, 0.0625, ((1, 32),)),
    }


def reference(acts, gate_weight):
    total = jnp.dot(acts.T, acts, preferred_element_type=jnp.float32)
    covariance = total / jnp.float32(TOKENS)
    gate_out = jnp.dot(acts, gate_weight, preferred_element_type=jnp.float32).astype(jnp.bfloat16)
    return covariance, gate_out
```

```python
import functools

import jax
import jax.numpy as jnp
from jax import lax
from jax.experimental import pallas as pl
from jax.experimental.pallas import tpu as pltpu
from jax.sharding import PartitionSpec as P

MESH = pl.DeviceIdType.MESH

ORDER = (
    (0, 0), (-1, 0), (0, -1), (0, 1), (1, 0), (0, -2), (0, 2), (1, 1),
    (1, -1), (0, -3), (0, 3), (1, 2), (2, 0), (1, -2), (0, 4), (-1, -1),
    (-1, 1), (1, 3), (1, -3), (2, -1), (-1, -2), (-1, 2), (1, 4), (-1, -3),
    (-1, 3), (2, -2), (2, 2), (2, -3), (2, 1), (-1, 4), (2, 3), (2, 4),
)

SENDS = (
    (-1, 0, 1, 0, 0, 2), (-1, 1, 1, 0, 0, 2), (-1, 2, 0, 0, 0, 2), (-1, 3, 0, 0, 0, 2),
    (-1, 2, 1, 0, 0, 2), (-1, 3, 1, 0, 0, 2), (-1, 0, 0, 0, 0, 2), (-1, 1, 0, 0, 0, 2),
    (1, 2, 0, 0, -1, 2), (1, 3, 0, 0, 1, 2), (1, 0, 1, -1, 0, 0), (1, 1, 1, 1, 0, 1),
    (2, 0, 1, 0, 1, 2), (2, 2, 1, 0, -1, 2), (2, 3, 1, 0, 1, 2), (2, 1, 1, 0, -1, 2),
    (2, 0, 1, 0, -1, 2), (2, 1, 0, 1, 0, 1), (2, 3, 0, 1, 0, 2), (2, 1, 1, 0, 1, 2),
    (3, 2, 0, 1, 0, 2), (4, 2, 0, 0, -2, 2), (4, 3, 0, 0, 2, 2), (6, 0, 1, -1, 1, 0),
    (6, 1, 1, 0, 2, 2), (6, 2, 1, 0, -2, 2), (6, 3, 1, 0, 2, 2), (6, 0, 1, 0, -2, 2),
    (7, 1, 1, 0, -2, 2), (7, 2, 0, 0, -3, 0), (7, 3, 0, 1, 1, 2), (7, 0, 0, -1, 0, 0),
    (7, 0, 1, -1, -1, 0), (7, 0, 1, 0, 2, 2), (7, 1, 1, 1, -1, 1), (8, 2, 0, 1, -1, 2),
    (8, 3, 0, 0, 3, 1), (9, 2, 0, -1, 0, 2), (9, 3, 0, -1, 0, 2), (10, 2, 1, 0, -3, 0),
    (10, 3, 1, 0, 3, 1), (10, 1, 1, 0, 3, 2), (10, 0, 1, 0, -3, 2), (11, 1, 1, 0, -3, 2),
    (12, 3, 0, 1, 2, 2), (12, 2, 0, 2, 0, 2), (12, 3, 0, 2, 0, 2), (13, 2, 0, 1, -2, 2),
    (14, 0, 1, 0, 4, 2), (14, 1, 1, 0, 4, 2), (16, 2, 0, -1, -1, 2), (16, 3, 0, -1, 1, 2),
    (16, 0, 1, -1, -2, 0), (16, 1, 1, 1, 3, 1), (17, 0, 1, -1, -3, 0), (18, 2, 0, 1, -3, 0),
    (18, 3, 0, 1, 3, 1), (18, 0, 1, 0, 3, 2), (19, 1, 1, 1, -3, 1), (19, 2, 0, 2, -1, 2),
    (19, 3, 0, 2, 1, 2), (20, 1, 1, 1, -2, 1), (20, 0, 1, -1, 4, 0), (20, 0, 1, -1, 2, 0),
    (20, 1, 1, 1, 2, 1), (21, 1, 1, 1, 4, 1), (21, 2, 0, -1, -2, 2), (21, 3, 0, -1, 2, 2),
    (22, 1, 1, 1, 1, 1), (23, 2, 0, 2, -2, 2), (23, 3, 0, 2, 2, 2), (24, 2, 0, -1, -3, 0),
    (24, 3, 0, -1, 3, 1), (24, 0, 1, -1, 3, 0), (26, 2, 0, 2, -3, 0), (26, 3, 0, 2, 3, 1),
)

TOK, FEA, HID = 384, 256, 512
SPLIT = 160
PARTS = ((0, SPLIT), (SPLIT, TOK))
STEPS = len(ORDER)
HALF = FEA // 2
LAG = 4


def landed(send):
    _, link, part, dy, dz, rows = send
    dy += (-1, 1, 0, 0)[link]
    dz += (0, 0, -1, 1)[link]
    return part, (2 if dy == -2 else dy), (4 if dz == -4 else dz), rows


def rows_of(part, rows):
    start, stop = PARTS[part]
    middle = (start + stop) // 2
    lo = middle if rows == 1 else start
    hi = middle if rows == 0 else stop
    return pl.ds(lo, hi - lo)


def needed(part, dy, dz, rows):
    return [
        n
        for n, send in enumerate(SENDS)
        if landed(send)[:3] == (part, dy, dz)
        and (rows == 2 or landed(send)[3] in (2, rows))
    ]


def tree(step, lo, hi, emit):
    if hi - lo == 1:
        emit(lo)
        return
    mid = (lo + hi) // 2
    lax.cond(
        step < mid,
        lambda: tree(step, lo, mid, emit),
        lambda: tree(step, mid, hi, emit),
    )


def pick(step, values):
    out = jnp.int32(values[0])
    for n, value in enumerate(values[1:], 1):
        out = jnp.where(step == n, jnp.int32(value), out)
    return out


def kernel(
    tokens, acts, weight, cov, gate,
    held, own_t, panel, total, part_sum, from_core, through, from_low, from_high,
    ag_send, ag_recv, core_send, core_recv, x_send, thr_recv, low_recv, high_recv, w_sem,
):
    dp, ten = lax.axis_index("dp"), lax.axis_index("tensor")
    x, core = dp // 2, dp % 2
    z, y = ten // 4, ten % 4

    def at(x_, core_, y_, z_):
        return (x_ * 2 + core_, z_ * 4 + y_)

    links = (
        at(x, core, (y + 1) % 4, z),
        at(x, core, (y + 3) % 4, z),
        at(x, core, y, (z + 1) % 8),
        at(x, core, y, (z + 7) % 8),
    )
    other = at(x, 1 - core, y, z)
    x_up = at((x + 1) % 4, core, y, z)
    x_down = at((x + 3) % 4, core, y, z)

    barrier = pltpu.get_barrier_semaphore()
    for device in (*links, other, x_up, x_down):
        pl.semaphore_signal(barrier, inc=1, device_id=device, device_id_type=MESH)

    w_copy = pltpu.make_async_copy(weight, panel, w_sem)
    w_copy.start()

    def block(dy, dz):
        return ((z + dz + 8) % 8) * 4 + (y + dy + 4) % 4

    held[block(0, 0)] = acts[...]
    pl.semaphore_wait(barrier, 7)

    def gather(n):
        _, link, part, dy, dz, rows = SENDS[n]
        ref = held.at[block(dy, dz), rows_of(part, rows)]
        return pltpu.make_async_remote_copy(
            src_ref=ref,
            dst_ref=ref,
            send_sem=ag_send.at[n],
            recv_sem=ag_recv.at[n],
            device_id=links[link],
            device_id_type=MESH,
        )

    def arrived(n):
        part, dy, dz, rows = landed(SENDS[n])
        ref = held.at[block(dy, dz), rows_of(part, rows)]
        pltpu.make_async_remote_copy(
            src_ref=ref,
            dst_ref=ref,
            send_sem=ag_send.at[n],
            recv_sem=ag_recv.at[n],
            device_id=links[SENDS[n][1]],
            device_id_type=MESH,
        ).wait_recv()

    events = [[] for _ in range(STEPS + 1)]
    seen = set()

    def want(step, receives):
        for n in receives:
            if n not in seen:
                seen.add(n)
                events[step + 1].append((arrived, n))

    for step in range(-1, STEPS):
        for n, send in enumerate(SENDS):
            if send[0] == step:
                want(step, needed(*send[2:]))
                events[step + 1].append((lambda m: gather(m).start(), n))
        if step >= 0:
            for part in range(2):
                want(step, needed(part, *ORDER[step], 2))

    def run(step):
        for action, n in events[step + 1]:
            action(n)

    run(-1)
    own_t[...] = acts[...].T
    total[...] = jnp.zeros_like(total)
    w_copy.wait()

    def where(step):
        dy = pick(step, [a for a, _ in ORDER])
        dz = pick(step, [b for _, b in ORDER])
        plane, col = (z + dz + 8) % 8, (y + dy + 4) % 4
        return plane * 4 + col, col, (plane // 2 - x + 4) % 4, plane % 2 == core

    def to_core(step):
        return pltpu.make_async_remote_copy(
            src_ref=part_sum.at[step],
            dst_ref=from_core.at[step],
            send_sem=core_send.at[step],
            recv_sem=core_recv.at[step],
            device_id=other,
            device_id_type=MESH,
        )

    def along_x(step, half, dst, recv_sem, device):
        return pltpu.make_async_remote_copy(
            src_ref=part_sum.at[step, pl.ds(half * HALF, HALF)],
            dst_ref=dst,
            send_sem=x_send.at[2 * step + half],
            recv_sem=recv_sem,
            device_id=device,
            device_id_type=MESH,
        )

    def thr(step, half, side, col, device):
        slot = 4 * side + col
        return along_x(step, half, through.at[slot], thr_recv.at[slot], device)

    def low(step, half, col):
        rows = pl.ds(half * HALF, HALF)
        return along_x(step, half, from_low.at[col, rows], low_recv.at[2 * col + half], x_up)

    def high(step, half, col):
        rows = pl.ds(half * HALF, HALF)
        return along_x(step, half, from_high.at[col, rows], high_recv.at[2 * col + half], x_down)

    def multiply(step):
        k, _, _, mine = where(step)
        part_sum[step] = jnp.dot(own_t[...], held[k], preferred_element_type=jnp.float32)

        @pl.when(jnp.logical_not(mine))
        def _():
            to_core(step).start()

        rows = pl.ds(pl.multiple_of(k * FEA, FEA), FEA)
        total[...] += jnp.dot(held[k], panel[rows, :], preferred_element_type=jnp.float32)

    def join(step):
        _, col, hops, mine = where(step)

        @pl.when(mine)
        def _():
            to_core(step).wait_recv()
            part_sum[step] += from_core[step]

            @pl.when(hops == 2)
            def _():
                thr(step, 0, 0, col, x_up).start()
                thr(step, 1, 1, col, x_down).start()

            @pl.when(hops == 1)
            def _():
                low(step, 1, col).start()

            @pl.when(hops == 3)
            def _():
                high(step, 0, col).start()

    def pass_on(step):
        _, col, hops, mine = where(step)

        @pl.when(mine & (hops == 1))
        def _():
            thr(step, 0, 0, col, x_up).wait_recv()
            part_sum[step, :HALF] += through[col]
            low(step, 0, col).start()

        @pl.when(mine & (hops == 3))
        def _():
            thr(step, 1, 1, col, x_down).wait_recv()
            part_sum[step, HALF:] += through[4 + col]
            high(step, 1, col).start()

    def finish(step):
        _, col, hops, mine = where(step)

        @pl.when(mine & (hops == 0))
        def _():
            for half in range(2):
                low(step, half, col).wait_recv()
                high(step, half, col).wait_recv()
            sums = part_sum[step] + (from_low[col] + from_high[col])
            cov[:, pl.ds(pl.multiple_of(col * FEA, FEA), FEA)] = sums / jnp.float32(tokens)

    def sent(step):
        _, col, hops, mine = where(step)

        @pl.when(jnp.logical_not(mine))
        def _():
            to_core(step).wait_send()

        @pl.when(mine & (hops != 0))
        def _():
            for half in range(2):
                low(step, half, col).wait_send()

    def step_body(step, _):
        @pl.when(step < STEPS)
        def _():
            tree(step, 0, STEPS, run)
            multiply(step)

        @pl.when((step >= 1) & (step < STEPS + 1))
        def _():
            join(step - 1)

        @pl.when(step >= LAG)
        def _():
            pass_on(step - LAG)

        return 0

    lax.fori_loop(0, STEPS + LAG, step_body, 0)
    gate[...] = total[...].astype(gate.dtype)

    def last_body(step, _):
        finish(step)
        return 0

    def sent_body(step, _):
        sent(step)
        return 0

    lax.fori_loop(0, STEPS, last_body, 0)
    lax.fori_loop(0, STEPS, sent_body, 0)
    for n in range(len(SENDS)):
        gather(n).wait_send()


def solution(mesh):
    def step(acts, weight):
        tokens = acts.shape[0] * mesh.shape["dp"]
        sems = pltpu.SemaphoreType.DMA
        f32, bf16 = jnp.float32, jnp.bfloat16
        return pl.pallas_call(
            functools.partial(kernel, tokens),
            out_shape=(
                jax.ShapeDtypeStruct((FEA, 4 * FEA), f32),
                jax.ShapeDtypeStruct((TOK, HID), bf16),
            ),
            in_specs=[
                pl.BlockSpec(memory_space=pltpu.VMEM),
                pl.BlockSpec(memory_space=pl.ANY),
            ],
            out_specs=[pl.BlockSpec(memory_space=pltpu.VMEM)] * 2,
            scratch_shapes=[
                pltpu.VMEM((32, TOK, FEA), bf16),
                pltpu.VMEM((FEA, TOK), bf16),
                pltpu.VMEM((32 * FEA, HID), bf16),
                pltpu.VMEM((TOK, HID), f32),
                pltpu.VMEM((STEPS, FEA, FEA), f32),
                pltpu.VMEM((STEPS, FEA, FEA), f32),
                pltpu.VMEM((8, HALF, FEA), f32),
                pltpu.VMEM((4, FEA, FEA), f32),
                pltpu.VMEM((4, FEA, FEA), f32),
                sems((len(SENDS),)),
                sems((len(SENDS),)),
                sems((STEPS,)),
                sems((STEPS,)),
                sems((2 * STEPS,)),
                sems((8,)),
                sems((8,)),
                sems((8,)),
                sems(()),
            ],
            compiler_params=pltpu.CompilerParams(
                collective_id=0, has_side_effects=True, vmem_limit_bytes=56 * 2**20
            ),
        )(acts, weight)

    return jax.shard_map(
        step,
        mesh=mesh,
        in_specs=(P("dp", "tensor"), P(None, "tensor")),
        out_specs=(P("tensor", "dp"), P("dp", "tensor")),
        check_vma=False,
    )
```

```python
import functools

import jax
import jax.numpy as jnp
from jax import lax
from jax.experimental import pallas as pl
from jax.experimental.pallas import tpu as pltpu
from jax.sharding import PartitionSpec as P

MESH = pl.DeviceIdType.MESH

ORDER = (
    (0, 0), (-1, 0), (0, -1), (0, 1), (1, 0), (-1, 1), (-1, -1), (0, -2),
    (0, 2), (-1, 2), (-1, -2), (0, -3), (0, 3), (1, 1), (1, -1), (0, 4),
    (-1, 3), (-1, -3), (1, -2), (1, 2), (2, 1), (-1, 4), (2, -1), (1, 3),
    (1, -3), (2, 2), (2, 0), (1, 4), (2, -2), (2, -3), (2, 3), (2, 4),
)

SENDS = (
    (-1, 0, 0, 0, 0, 2), (-1, 1, 0, 0, 0, 2), (-1, 2, 0, 0, 0, 2), (-1, 3, 1, 0, 0, 2),
    (-1, 0, 1, 0, 0, 2), (-1, 1, 1, 0, 0, 2), (-1, 2, 1, 0, 0, 2), (-1, 3, 0, 0, 0, 2),
    (1, 0, 0, -1, 0, 0), (1, 1, 0, 1, 0, 1), (1, 2, 0, -1, 0, 2), (1, 3, 0, -1, 0, 2),
    (1, 2, 0, 0, -1, 2), (1, 0, 1, 0, 1, 2), (1, 1, 1, 0, 1, 2), (1, 3, 1, 0, 1, 2),
    (2, 0, 1, 0, -1, 2), (2, 1, 1, 0, -1, 2), (2, 2, 1, 0, -1, 2), (3, 3, 0, 0, 1, 2),
    (4, 3, 0, -1, 1, 2), (5, 2, 0, -1, -1, 2), (5, 0, 1, -1, 1, 0), (5, 1, 1, 1, 1, 1),
    (6, 2, 0, 0, -2, 2), (6, 0, 1, 0, 2, 2), (6, 1, 1, 0, 2, 2), (6, 3, 1, 0, 2, 2),
    (7, 0, 1, 0, -2, 2), (7, 1, 1, 0, -2, 2), (7, 2, 1, 0, -2, 2), (8, 3, 0, 1, 0, 2),
    (9, 3, 0, 0, 2, 2), (9, 2, 0, 0, -3, 0), (9, 2, 0, 1, 0, 2), (10, 0, 1, -1, 2, 0),
    (10, 1, 1, 1, 2, 1), (10, 0, 1, 0, 3, 2), (10, 1, 1, 0, 3, 2), (10, 3, 1, 0, 3, 1),
    (10, 1, 1, 1, 0, 1), (10, 2, 0, -1, -2, 2), (10, 3, 0, -1, 2, 2), (11, 2, 1, 0, -3, 0),
    (11, 0, 1, 0, -3, 2), (11, 1, 1, 1, -2, 1), (11, 3, 0, 0, 3, 1), (12, 0, 1, -1, -1, 0),
    (13, 3, 0, 1, 1, 2), (13, 2, 0, 2, 0, 2), (13, 3, 0, 2, 0, 2), (14, 2, 0, 1, -1, 2),
    (15, 1, 1, 1, 3, 1), (15, 0, 1, 0, 4, 2), (15, 1, 1, 0, 4, 2), (16, 1, 1, 1, -1, 1),
    (17, 2, 0, -1, -3, 0), (17, 3, 0, -1, 3, 1), (17, 0, 1, -1, 3, 0), (17, 1, 1, 0, -3, 2),
    (17, 0, 1, -1, -3, 0), (19, 2, 0, 1, -2, 2), (19, 3, 0, 1, 2, 2), (20, 0, 1, -1, 0, 0),
    (21, 2, 0, 2, -1, 2), (21, 3, 0, 2, 1, 2), (21, 0, 1, -1, -2, 0), (21, 0, 1, -1, 4, 0),
    (21, 1, 1, 1, 4, 1), (23, 2, 0, 1, -3, 0), (23, 3, 0, 1, 3, 1), (25, 1, 1, 1, -3, 1),
    (25, 2, 0, 2, -2, 2), (25, 3, 0, 2, 2, 2), (29, 2, 0, 2, -3, 0), (29, 3, 0, 2, 3, 1),
)

TOK, FEA, HID = 384, 256, 512
SPLIT = 160
PARTS = ((0, SPLIT), (SPLIT, TOK))
STEPS = len(ORDER)
HALF = FEA // 2
LAG = 8
GATE_LAG = 8
END_LAG = 15
CODED = HALF + HALF // 2


def landed(send):
    _, link, part, dy, dz, rows = send
    dy += (-1, 1, 0, 0)[link]
    dz += (0, 0, -1, 1)[link]
    return part, (2 if dy == -2 else dy), (4 if dz == -4 else dz), rows


def rows_of(part, rows):
    start, stop = PARTS[part]
    middle = (start + stop) // 2
    lo = middle if rows == 1 else start
    hi = middle if rows == 0 else stop
    return pl.ds(lo, hi - lo)


def needed(part, dy, dz, rows):
    return [
        n
        for n, send in enumerate(SENDS)
        if landed(send)[:3] == (part, dy, dz)
        and (rows == 2 or landed(send)[3] in (2, rows))
    ]


def tree(step, lo, hi, emit):
    if hi - lo == 1:
        emit(lo)
        return
    mid = (lo + hi) // 2
    lax.cond(
        step < mid,
        lambda: tree(step, lo, mid, emit),
        lambda: tree(step, mid, hi, emit),
    )


def pick(step, values):
    out = jnp.int32(values[0])
    for n, value in enumerate(values[1:], 1):
        out = jnp.where(step == n, jnp.int32(value), out)
    return out


def encode(sums, ref):
    head = sums.astype(jnp.bfloat16)
    wide = head.astype(jnp.float32)
    usable = jnp.abs(wide) > 1e-37
    inverse = pl.reciprocal(jnp.where(usable, wide, 1.0), approx=True)
    ratio = jnp.where(usable, (sums - wide) * inverse, 0.0)
    level = jnp.clip(jnp.floor(ratio * 2048.0 + 8.0), 0.0, 15.0)
    quarter = HALF // 2
    ref[:HALF] = head
    ref[HALF:] = (level[:quarter] * 16.0 + level[quarter:]).astype(jnp.bfloat16)


def decode(ref):
    wide = ref[:HALF].astype(jnp.float32)
    pair = ref[HALF:].astype(jnp.float32)
    upper = jnp.floor(pair * 0.0625)
    level = jnp.concatenate([upper, pair - upper * 16.0], axis=0)
    return wide + wide * ((level - 7.5) * (1.0 / 2048.0))


def kernel(
    tokens, acts, weight, cov, gate,
    held, own_t, panel, total, part_sum, coded, through, from_low, from_high, cov_buf, gate_buf,
    ag_send, ag_recv, core_send, core_recv, x_send, thr_recv, low_recv, high_recv, w_sem, a_sem, out_sem,
):
    dp, ten = lax.axis_index("dp"), lax.axis_index("tensor")
    x, core = dp // 2, dp % 2
    z, y = ten // 4, ten % 4

    def at(x_, core_, y_, z_):
        return (x_ * 2 + core_, z_ * 4 + y_)

    links = (
        at(x, core, (y + 1) % 4, z),
        at(x, core, (y + 3) % 4, z),
        at(x, core, y, (z + 1) % 8),
        at(x, core, y, (z + 7) % 8),
    )
    other = at(x, 1 - core, y, z)
    x_up = at((x + 1) % 4, core, y, z)
    x_down = at((x + 3) % 4, core, y, z)

    def block(dy, dz):
        return ((z + dz + 8) % 8) * 4 + (y + dy + 4) % 4

    own = block(0, 0)
    barrier = pltpu.get_barrier_semaphore()
    for device in (*links, other, x_up, x_down):
        pl.semaphore_signal(barrier, inc=1, device_id=device, device_id_type=MESH)
    a_copy = pltpu.make_async_copy(acts, held.at[own, pl.ds(0, TOK)], a_sem)
    a_copy.start()
    w_copy = pltpu.make_async_copy(weight, panel, w_sem)
    w_copy.start()
    total[...] = jnp.zeros_like(total)
    a_copy.wait()
    pl.semaphore_wait(barrier, 7)

    def gather(n):
        _, link, part, dy, dz, rows = SENDS[n]
        ref = held.at[block(dy, dz), rows_of(part, rows)]
        return pltpu.make_async_remote_copy(
            src_ref=ref,
            dst_ref=ref,
            send_sem=ag_send.at[n],
            recv_sem=ag_recv.at[n],
            device_id=links[link],
            device_id_type=MESH,
        )

    def arrived(n):
        part, dy, dz, rows = landed(SENDS[n])
        ref = held.at[block(dy, dz), rows_of(part, rows)]
        pltpu.make_async_remote_copy(
            src_ref=ref,
            dst_ref=ref,
            send_sem=ag_send.at[n],
            recv_sem=ag_recv.at[n],
            device_id=links[SENDS[n][1]],
            device_id_type=MESH,
        ).wait_recv()

    events = [[] for _ in range(STEPS + 1)]
    seen = set()

    def want(step, receives):
        for n in receives:
            if n not in seen:
                seen.add(n)
                events[step + 1].append((arrived, n))

    for step in range(-1, STEPS):
        for n, send in enumerate(SENDS):
            if send[0] == step:
                want(step, needed(*send[2:]))
                events[step + 1].append((lambda m: gather(m).start(), n))
        if step >= 0:
            for part in range(2):
                want(step, needed(part, *ORDER[step], 2))

    def run(step):
        for action, n in events[step + 1]:
            action(n)

    def where(step):
        dy = pick(step, [a for a, _ in ORDER])
        dz = pick(step, [b for _, b in ORDER])
        plane, col = (z + dz + 8) % 8, (y + dy + 4) % 4
        return plane * 4 + col, col, (plane // 2 - x + 4) % 4, plane % 2 == core

    def to_core(step, k):
        return pltpu.make_async_remote_copy(
            src_ref=held.at[k, pl.ds(0, TOK)],
            dst_ref=held.at[k, pl.ds(TOK, TOK)],
            send_sem=core_send.at[step],
            recv_sem=core_recv.at[step],
            device_id=other,
            device_id_type=MESH,
        )

    def along_x(step, half, dst, recv_sem, device):
        return pltpu.make_async_remote_copy(
            src_ref=coded.at[step, half],
            dst_ref=dst,
            send_sem=x_send.at[2 * step + half],
            recv_sem=recv_sem,
            device_id=device,
            device_id_type=MESH,
        )

    def thr(step, half, side, col, device):
        slot = 4 * side + col
        return along_x(step, half, through.at[slot], thr_recv.at[slot], device)

    def low(step, half, col):
        return along_x(step, half, from_low.at[2 * col + half], low_recv.at[2 * col + half], x_up)

    def high(step, half, col):
        return along_x(step, half, from_high.at[2 * col + half], high_recv.at[2 * col + half], x_down)

    def share(step):
        k, _, _, mine = where(step)

        @pl.when(jnp.logical_not(mine) | (step == 0))
        def _():
            to_core(step, k).start()

    def partial(step):
        k, col, hops, mine = where(step)

        @pl.when(mine)
        def _():
            @pl.when(step > 0)
            def _():
                to_core(step, k).wait_recv()

            part_sum[step] = jnp.dot(own_t[...], held[k], preferred_element_type=jnp.float32)

            @pl.when((hops == 2) | (hops == 3))
            def _():
                encode(part_sum[step, :HALF], coded.at[step, 0])

            @pl.when(hops == 2)
            def _():
                thr(step, 0, 0, col, x_up).start()

            @pl.when(hops == 3)
            def _():
                high(step, 0, col).start()

            @pl.when((hops == 2) | (hops == 1))
            def _():
                encode(part_sum[step, HALF:], coded.at[step, 1])

            @pl.when(hops == 2)
            def _():
                thr(step, 1, 1, col, x_down).start()

            @pl.when(hops == 1)
            def _():
                low(step, 1, col).start()

    def pass_on(step):
        _, col, hops, mine = where(step)

        @pl.when(mine & (hops == 1))
        def _():
            thr(step, 0, 0, col, x_up).wait_recv()
            encode(part_sum[step, :HALF] + decode(through.at[col]), coded.at[step, 0])
            low(step, 0, col).start()

        @pl.when(mine & (hops == 3))
        def _():
            thr(step, 1, 1, col, x_down).wait_recv()
            encode(part_sum[step, HALF:] + decode(through.at[4 + col]), coded.at[step, 1])
            high(step, 1, col).start()

    def project(step):
        k, _, _, _ = where(step)
        rows = pl.ds(pl.multiple_of(k * FEA, FEA), FEA)
        total[...] += jnp.dot(held[k, :TOK], panel[rows, :], preferred_element_type=jnp.float32)

    def out_copy(col):
        columns = pl.ds(pl.multiple_of(col * FEA, FEA), FEA)
        return pltpu.make_async_copy(cov_buf.at[col], cov.at[:, columns], out_sem.at[col])

    def finish(step):
        _, col, hops, mine = where(step)

        @pl.when(mine & (hops == 0))
        def _():
            for half in range(2):
                low(step, half, col).wait_recv()
                high(step, half, col).wait_recv()
                slot = 2 * col + half
                rows = pl.ds(half * HALF, HALF)
                sums = part_sum[step, rows] + (decode(from_low.at[slot]) + decode(from_high.at[slot]))
                cov_buf[col, rows] = sums / jnp.float32(tokens)
            out_copy(col).start()

    def sent(step):
        k, col, hops, mine = where(step)

        @pl.when(jnp.logical_not(mine) | (step == 0))
        def _():
            to_core(step, k).wait_send()

        @pl.when(mine & (hops != 0))
        def _():
            for half in range(2):
                low(step, half, col).wait_send()

    run(-1)
    share(0)
    own_t[:, :TOK] = held[own, :TOK].T
    to_core(0, own).wait_recv()
    own_t[:, TOK:] = held[own, TOK:].T
    w_copy.wait()

    def step_body(step, _):
        @pl.when(step < STEPS)
        def _():
            tree(step, 0, STEPS, run)

        @pl.when((step > 0) & (step < STEPS))
        def _():
            share(step)

        @pl.when((step >= 1) & (step < STEPS + 1))
        def _():
            partial(step - 1)

        @pl.when(step >= LAG)
        def _():
            pass_on(step - LAG)

        @pl.when(step >= GATE_LAG)
        def _():
            project(step - GATE_LAG)

        @pl.when(step >= END_LAG)
        def _():
            finish(step - END_LAG)

        return 0

    lax.fori_loop(0, STEPS + LAG, step_body, 0)
    gate_buf[...] = total[...].astype(gate.dtype)
    gate_copy = pltpu.make_async_copy(gate_buf, gate, a_sem)
    gate_copy.start()

    def last_body(step, _):
        finish(step)
        return 0

    def sent_body(step, _):
        sent(step)
        return 0

    lax.fori_loop(0, STEPS, sent_body, 0)
    for n in range(len(SENDS)):
        gather(n).wait_send()
    lax.fori_loop(STEPS + LAG - END_LAG, STEPS, last_body, 0)
    gate_copy.wait()
    for col in range(4):
        out_copy(col).wait()


def solution(mesh):
    def step(acts, weight):
        tokens = acts.shape[0] * mesh.shape["dp"]
        sems = pltpu.SemaphoreType.DMA
        f32, bf16 = jnp.float32, jnp.bfloat16
        return pl.pallas_call(
            functools.partial(kernel, tokens),
            out_shape=(
                jax.ShapeDtypeStruct((FEA, 4 * FEA), f32),
                jax.ShapeDtypeStruct((TOK, HID), bf16),
            ),
            in_specs=[pl.BlockSpec(memory_space=pl.ANY)] * 2,
            out_specs=[pl.BlockSpec(memory_space=pl.ANY)] * 2,
            scratch_shapes=[
                pltpu.VMEM((32, 2 * TOK, FEA), bf16),
                pltpu.VMEM((FEA, 2 * TOK), bf16),
                pltpu.VMEM((32 * FEA, HID), bf16),
                pltpu.VMEM((TOK, HID), f32),
                pltpu.VMEM((STEPS, FEA, FEA), f32),
                pltpu.VMEM((STEPS, 2, CODED, FEA), bf16),
                pltpu.VMEM((8, CODED, FEA), bf16),
                pltpu.VMEM((8, CODED, FEA), bf16),
                pltpu.VMEM((8, CODED, FEA), bf16),
                pltpu.VMEM((4, FEA, FEA), f32),
                pltpu.VMEM((TOK, HID), bf16),
                sems((len(SENDS),)),
                sems((len(SENDS),)),
                sems((STEPS,)),
                sems((STEPS,)),
                sems((2 * STEPS,)),
                sems((8,)),
                sems((8,)),
                sems((8,)),
                sems(()),
                sems(()),
                sems((4,)),
            ],
            compiler_params=pltpu.CompilerParams(
                collective_id=0, has_side_effects=True, vmem_limit_bytes=56 * 2**20
            ),
        )(acts, weight)

    return jax.shard_map(
        step,
        mesh=mesh,
        in_specs=(P("dp", "tensor"), P(None, "tensor")),
        out_specs=(P("tensor", "dp"), P("dp", "tensor")),
        check_vma=False,
    )
```

```python
import functools

import jax
import jax.numpy as jnp
from jax import lax
from jax.experimental import pallas as pl
from jax.experimental.pallas import tpu as pltpu
from jax.sharding import PartitionSpec as P

MESH = pl.DeviceIdType.MESH

ORDER = (
    (0, 0), (-1, 0), (0, -1), (0, 1), (1, 0), (1, 1), (1, -1), (-1, 1),
    (0, -2), (0, 2), (2, 0), (-1, -1), (-1, 2), (0, 3), (-1, -2), (0, -3),
    (1, -2), (-1, 3), (2, 1), (-1, -3), (1, 2), (0, 4), (2, -2), (2, 2),
    (1, 3), (1, -3), (-1, 4), (2, -3), (2, 3), (2, -1), (1, 4), (2, 4),
)

SENDS = (
    (-1, 0, 1, 0, 0, 2), (-1, 1, 0, 0, 0, 2), (-1, 2, 0, 0, 0, 2), (-1, 3, 1, 0, 0, 2),
    (-1, 1, 1, 0, 0, 2), (-1, 2, 1, 0, 0, 2), (-1, 0, 0, 0, 0, 2), (-1, 3, 0, 0, 0, 2),
    (1, 1, 0, 1, 0, 1), (1, 2, 0, 0, -1, 2), (1, 3, 0, 1, 0, 2), (1, 2, 0, 1, 0, 2),
    (1, 0, 1, -1, 0, 0), (1, 1, 1, 0, 1, 2), (1, 3, 1, 0, 1, 2), (1, 0, 1, 0, 1, 2),
    (2, 1, 1, 0, -1, 2), (2, 2, 1, 0, -1, 2), (2, 0, 1, 0, -1, 2), (2, 3, 0, -1, 0, 2),
    (3, 1, 1, 1, 0, 1), (3, 3, 0, 0, 1, 2), (5, 2, 0, -1, 0, 2), (5, 0, 0, -1, 0, 0),
    (6, 2, 0, 1, -1, 2), (6, 1, 1, 0, 2, 2), (6, 3, 1, 0, 2, 2), (6, 0, 1, 0, 2, 2),
    (6, 0, 1, -1, 1, 0), (6, 1, 1, 1, 1, 1), (7, 1, 1, 1, -1, 1), (7, 3, 0, -1, 1, 2),
    (7, 2, 1, 0, -2, 2), (7, 0, 1, 0, -2, 2), (10, 3, 0, 0, 2, 2), (10, 1, 1, 0, -2, 2),
    (10, 2, 0, 0, -2, 2), (12, 1, 1, 1, 2, 1), (12, 2, 0, -1, -1, 2), (12, 3, 1, 0, 3, 1),
    (12, 0, 1, 0, 3, 2), (12, 2, 0, 2, 0, 2), (12, 3, 0, 2, 0, 2), (13, 1, 1, 0, -3, 2),
    (13, 0, 1, 0, -3, 2), (13, 3, 0, -1, 2, 2), (13, 3, 0, 1, 1, 2), (14, 2, 0, -1, -2, 2),
    (14, 0, 1, -1, 2, 0), (15, 1, 1, 0, 3, 2), (15, 2, 1, 0, -3, 0), (15, 0, 1, -1, -2, 0),
    (15, 3, 0, 0, 3, 1), (16, 2, 0, 0, -3, 0), (16, 1, 1, 1, -2, 1), (17, 0, 1, -1, 3, 0),
    (18, 2, 0, 2, -1, 2), (18, 1, 1, 1, -3, 1), (18, 3, 0, 2, 1, 2), (19, 0, 1, -1, -3, 0),
    (19, 2, 0, 1, -2, 2), (19, 2, 0, -1, -3, 0), (20, 3, 0, -1, 3, 1), (21, 3, 0, 1, 2, 2),
    (22, 1, 1, 0, 4, 2), (22, 0, 1, 0, 4, 2), (22, 0, 1, -1, -1, 0), (22, 1, 1, 1, 3, 1),
    (22, 2, 0, 2, -2, 2), (22, 3, 0, 2, 2, 2), (25, 3, 0, 1, 3, 1), (26, 2, 0, 1, -3, 0),
    (26, 1, 1, 1, 4, 1), (26, 0, 1, -1, 4, 0), (27, 2, 0, 2, -3, 0), (27, 3, 0, 2, 3, 1),
)

TOK, FEA, HID = 384, 256, 512
SPLIT = 160
PARTS = ((0, SPLIT), (SPLIT, TOK))
STEPS = len(ORDER)
HALF = FEA // 2
LAG = 6
GATE_LAG = 12
END_LAG = 20
MOST = max(LAG, GATE_LAG - 3)
SCALE = 256 * 5.45
CODED = HALF + HALF // 4


def landed(send):
    _, link, part, dy, dz, rows = send
    dy += (-1, 1, 0, 0)[link]
    dz += (0, 0, -1, 1)[link]
    return part, (2 if dy == -2 else dy), (4 if dz == -4 else dz), rows


def rows_of(part, rows):
    start, stop = PARTS[part]
    middle = (start + stop) // 2
    lo = middle if rows == 1 else start
    hi = middle if rows == 0 else stop
    return pl.ds(lo, hi - lo)


def needed(part, dy, dz, rows):
    return [
        n
        for n, send in enumerate(SENDS)
        if landed(send)[:3] == (part, dy, dz)
        and (rows == 2 or landed(send)[3] in (2, rows))
    ]


def tree(step, lo, hi, emit):
    if hi - lo == 1:
        emit(lo)
        return
    mid = (lo + hi) // 2
    lax.cond(
        step < mid,
        lambda: tree(step, lo, mid, emit),
        lambda: tree(step, mid, hi, emit),
    )


WORDS = tuple(
    sum((dy + 1 + 4 * (dz + 3)) << (5 * n) for n, (dy, dz) in enumerate(ORDER[w : w + 6]))
    for w in range(0, STEPS, 6)
)


def offsets(step):
    word = jnp.int32(WORDS[0])
    for n, value in enumerate(WORDS[1:], 1):
        word = jnp.where(step >= 6 * n, jnp.int32(value), word)
    bits = lax.shift_right_logical(word, 5 * lax.rem(step, 6)) & 31
    return (bits & 3) - 1, lax.shift_right_logical(bits, 2) - 3


def encode(sums, ref):
    head = sums.astype(jnp.bfloat16)
    wide = head.astype(jnp.float32)
    inverse = pl.reciprocal(jnp.where(jnp.abs(wide) > 1e-37, wide, 1.0), approx=True)
    level = jnp.floor(((sums - wide) * SCALE) * inverse + 5.5)
    q = HALF // 4
    code = (level[:q] + level[q : 2 * q] * 11.0) + (level[2 * q : 3 * q] * 121.0 + level[3 * q :] * 1331.0)
    power = jnp.floor(code * (1.0 / 256.0))
    rest = code - power * 256.0
    place = jnp.where(rest >= 128.0, -rest, rest + 128.0)
    ref[:HALF] = head
    ref[HALF:] = (place * jnp.exp2(power)).astype(jnp.bfloat16)


def decode(ref):
    wide = ref[:HALF].astype(jnp.float32)
    place = ref[HALF:].astype(jnp.float32)
    size = jnp.abs(place)
    power = jnp.floor(jnp.log2(size * 1.002)) - 7.0
    size = jnp.floor(size * jnp.exp2(-power) + 0.5)
    code = power * 256.0 + jnp.where(place < 0.0, size, size - 128.0)
    one = jnp.floor((code + 0.5) * (1.0 / 1331.0))
    code = code - one * 1331.0
    two = jnp.floor((code + 0.5) * (1.0 / 121.0))
    code = code - two * 121.0
    three = jnp.floor((code + 0.5) * (1.0 / 11.0))
    level = jnp.concatenate([code - three * 11.0, three, two, one], axis=0)
    return wide + wide * ((level - 5.0) * (1.0 / SCALE))


def kernel(
    tokens, acts, weight, cov, gate,
    held, own_t, panel, total, part_sum, coded, through, from_low, from_high,
    ag_send, ag_recv, core_send, core_recv, x_send, thr_recv, low_recv, high_recv, w_sem, a_sem,
):
    dp, ten = lax.axis_index("dp"), lax.axis_index("tensor")
    x, core = dp // 2, dp % 2
    z, y = ten // 4, ten % 4

    def at(x_, core_, y_, z_):
        return (x_ * 2 + core_, z_ * 4 + y_)

    links = (
        at(x, core, (y + 1) % 4, z),
        at(x, core, (y + 3) % 4, z),
        at(x, core, y, (z + 1) % 8),
        at(x, core, y, (z + 7) % 8),
    )
    other = at(x, 1 - core, y, z)
    x_up = at((x + 1) % 4, core, y, z)
    x_down = at((x + 3) % 4, core, y, z)

    def block(dy, dz):
        return ((z + dz + 8) % 8) * 4 + (y + dy + 4) % 4

    own = block(0, 0)
    barrier = pltpu.get_barrier_semaphore()
    for device in (*links, other, x_up, x_down):
        pl.semaphore_signal(barrier, inc=1, device_id=device, device_id_type=MESH)
    a_copy = pltpu.make_async_copy(acts, held.at[own, pl.ds(0, TOK)], a_sem)
    a_copy.start()
    w_copy = pltpu.make_async_copy(weight, panel, w_sem)
    w_copy.start()
    total[...] = jnp.zeros_like(total)
    pl.semaphore_wait(barrier, 7)

    def gather(n):
        _, link, part, dy, dz, rows = SENDS[n]
        ref = held.at[block(dy, dz), rows_of(part, rows)]
        return pltpu.make_async_remote_copy(
            src_ref=acts.at[rows_of(part, rows)] if dy == dz == 0 else ref,
            dst_ref=ref,
            send_sem=ag_send.at[n],
            recv_sem=ag_recv.at[n],
            device_id=links[link],
            device_id_type=MESH,
        )

    def arrived(n):
        part, dy, dz, rows = landed(SENDS[n])
        ref = held.at[block(dy, dz), rows_of(part, rows)]
        pltpu.make_async_remote_copy(
            src_ref=ref,
            dst_ref=ref,
            send_sem=ag_send.at[n],
            recv_sem=ag_recv.at[n],
            device_id=links[SENDS[n][1]],
            device_id_type=MESH,
        ).wait_recv()

    events = [[] for _ in range(STEPS + 1)]
    seen = set()

    def want(step, receives):
        for n in receives:
            if n not in seen:
                seen.add(n)
                events[step + 1].append((arrived, n))

    for step in range(-1, STEPS):
        for n, send in enumerate(SENDS):
            if send[0] == step:
                want(step, needed(*send[2:]))
                events[step + 1].append((lambda m: gather(m).start(), n))
        if step >= 0:
            for part in range(2):
                want(step, needed(part, *ORDER[step], 2))

    def run(step):
        for action, n in events[step + 1]:
            action(n)

    def where(step):
        dy, dz = offsets(step)
        plane, col = (z + dz + 8) & 7, (y + dy + 4) & 3
        hops = (lax.shift_right_logical(plane, 1) - x + 4) & 3
        return plane * 4 + col, col, hops, (plane & 1) == core

    def to_core(step, k):
        return pltpu.make_async_remote_copy(
            src_ref=held.at[k, pl.ds(0, TOK)],
            dst_ref=held.at[k, pl.ds(TOK, TOK)],
            send_sem=core_send.at[step],
            recv_sem=core_recv.at[step],
            device_id=other,
            device_id_type=MESH,
        )

    def along_x(step, half, dst, recv_sem, device):
        return pltpu.make_async_remote_copy(
            src_ref=coded.at[step, half],
            dst_ref=dst,
            send_sem=x_send.at[2 * step + half],
            recv_sem=recv_sem,
            device_id=device,
            device_id_type=MESH,
        )

    def thr(step, half, side, col, device):
        slot = 4 * side + col
        return along_x(step, half, through.at[slot], thr_recv.at[slot], device)

    def low(step, half, col):
        return along_x(step, half, from_low.at[2 * col + half], low_recv.at[2 * col + half], x_up)

    def high(step, half, col):
        return along_x(step, half, from_high.at[2 * col + half], high_recv.at[2 * col + half], x_down)

    def share(step):
        k, _, _, mine = where(step)

        @pl.when(jnp.logical_not(mine) | (step == 0))
        def _():
            to_core(step, k).start()

    def partial(step):
        k, col, hops, mine = where(step)

        @pl.when(mine)
        def _():
            @pl.when(step > 0)
            def _():
                to_core(step, k).wait_recv()

            part_sum[step] = jnp.dot(own_t[...], held[k], preferred_element_type=jnp.float32)

            @pl.when((hops == 2) | (hops == 3))
            def _():
                encode(part_sum[step, :HALF], coded.at[step, 0])

            @pl.when(hops == 2)
            def _():
                thr(step, 0, 0, col, x_up).start()

            @pl.when(hops == 3)
            def _():
                high(step, 0, col).start()

            @pl.when((hops == 2) | (hops == 1))
            def _():
                encode(part_sum[step, HALF:], coded.at[step, 1])

            @pl.when(hops == 2)
            def _():
                thr(step, 1, 1, col, x_down).start()

            @pl.when(hops == 1)
            def _():
                low(step, 1, col).start()

    def pass_on(step):
        _, col, hops, mine = where(step)

        @pl.when(mine & (hops == 1))
        def _():
            thr(step, 0, 0, col, x_up).wait_recv()
            encode(part_sum[step, :HALF] + decode(through.at[col]), coded.at[step, 0])
            low(step, 0, col).start()

        @pl.when(mine & (hops == 3))
        def _():
            thr(step, 1, 1, col, x_down).wait_recv()
            encode(part_sum[step, HALF:] + decode(through.at[4 + col]), coded.at[step, 1])
            high(step, 1, col).start()

    def product(step):
        k, _, _, _ = where(step)
        rows = pl.ds(pl.multiple_of(k * FEA, FEA), FEA)
        return jnp.dot(held[k, :TOK], panel[rows, :], preferred_element_type=jnp.float32)

    def project(step):
        total[...] += (product(step) + product(step + 1)) + (product(step + 2) + product(step + 3))

    def finish(step):
        _, col, hops, mine = where(step)

        @pl.when(mine & (hops == 0))
        def _():
            for half in range(2):
                low(step, half, col).wait_recv()
                high(step, half, col).wait_recv()
                slot = 2 * col + half
                rows = pl.ds(half * HALF, HALF)
                sums = part_sum[step, rows] + (decode(from_low.at[slot]) + decode(from_high.at[slot]))
                columns = pl.ds(pl.multiple_of(col * FEA, FEA), FEA)
                cov[rows, columns] = sums / jnp.float32(tokens)

    def sent(step):
        k, col, hops, mine = where(step)

        @pl.when(jnp.logical_not(mine) | (step == 0))
        def _():
            to_core(step, k).wait_send()

        @pl.when(mine & (hops != 0))
        def _():
            for half in range(2):
                low(step, half, col).wait_send()

    run(-1)
    a_copy.wait()
    share(0)
    own_t[:, :TOK] = held[own, :TOK].T
    to_core(0, own).wait_recv()
    own_t[:, TOK:] = held[own, TOK:].T
    w_copy.wait()

    def step_body(step, _):
        @pl.when(step < STEPS)
        def _():
            tree(step, 0, STEPS, run)

        @pl.when((step > 0) & (step < STEPS))
        def _():
            share(step)

        @pl.when((step >= 1) & (step < STEPS + 1))
        def _():
            partial(step - 1)

        @pl.when((step >= LAG) & (step < STEPS + LAG))
        def _():
            pass_on(step - LAG)

        @pl.when((step >= GATE_LAG) & (step % 4 == GATE_LAG % 4))
        def _():
            project(step - GATE_LAG)

        @pl.when(step >= END_LAG)
        def _():
            finish(step - END_LAG)

        return 0

    lax.fori_loop(0, STEPS + MOST, step_body, 0)
    gate[...] = total[...].astype(gate.dtype)

    def last_body(step, _):
        finish(step)
        return 0

    def sent_body(step, _):
        sent(step)
        return 0

    lax.fori_loop(0, STEPS, sent_body, 0)
    for n in range(len(SENDS)):
        gather(n).wait_send()
    lax.fori_loop(STEPS + MOST - END_LAG, STEPS, last_body, 0)


def solution(mesh):
    def step(acts, weight):
        tokens = acts.shape[0] * mesh.shape["dp"]
        sems = pltpu.SemaphoreType.DMA
        f32, bf16 = jnp.float32, jnp.bfloat16
        return pl.pallas_call(
            functools.partial(kernel, tokens),
            out_shape=(
                pltpu.VMEM((FEA, 4 * FEA), f32),
                pltpu.VMEM((TOK, HID), bf16),
            ),
            in_specs=[pl.BlockSpec(memory_space=pl.ANY)] * 2,
            out_specs=[pl.BlockSpec(memory_space=pltpu.VMEM)] * 2,
            scratch_shapes=[
                pltpu.VMEM((32, 2 * TOK, FEA), bf16),
                pltpu.VMEM((FEA, 2 * TOK), bf16),
                pltpu.VMEM((32 * FEA, HID), bf16),
                pltpu.VMEM((TOK, HID), f32),
                pltpu.VMEM((STEPS, FEA, FEA), f32),
                pltpu.VMEM((STEPS, 2, CODED, FEA), bf16),
                pltpu.VMEM((8, CODED, FEA), bf16),
                pltpu.VMEM((8, CODED, FEA), bf16),
                pltpu.VMEM((8, CODED, FEA), bf16),
                sems((len(SENDS),)),
                sems((len(SENDS),)),
                sems((STEPS,)),
                sems((STEPS,)),
                sems((2 * STEPS,)),
                sems((8,)),
                sems((8,)),
                sems((8,)),
                sems(()),
                sems(()),
            ],
            compiler_params=pltpu.CompilerParams(
                collective_id=0, has_side_effects=True, vmem_limit_bytes=56 * 2**20
            ),
        )(acts, weight)

    return jax.shard_map(
        step,
        mesh=mesh,
        in_specs=(P("dp", "tensor"), P(None, "tensor")),
        out_specs=(P("tensor", "dp"), P("dp", "tensor")),
        check_vma=False,
    )
```

```python
import functools

import jax
import jax.numpy as jnp
from jax import lax
from jax.experimental import pallas as pl
from jax.experimental.pallas import tpu as pltpu
from jax.sharding import PartitionSpec as P

MESH = pl.DeviceIdType.MESH

ORDER = (
    (0, 0), (-1, 0), (0, -1), (0, 1), (1, 0), (1, 1), (1, -1), (-1, 1),
    (0, -2), (0, 2), (2, 0), (-1, -1), (-1, 2), (0, 3), (-1, -2), (0, -3),
    (1, -2), (-1, 3), (2, 1), (-1, -3), (1, 2), (0, 4), (2, -2), (2, 2),
    (1, 3), (1, -3), (-1, 4), (2, -3), (2, 3), (2, -1), (1, 4), (2, 4),
)

SENDS = (
    (-1, 0, 1, 0, 0, 2), (-1, 1, 0, 0, 0, 2), (-1, 2, 0, 0, 0, 2), (-1, 3, 1, 0, 0, 2),
    (-1, 1, 1, 0, 0, 2), (-1, 2, 1, 0, 0, 2), (-1, 0, 0, 0, 0, 2), (-1, 3, 0, 0, 0, 2),
    (1, 1, 0, 1, 0, 1), (1, 2, 0, 0, -1, 2), (1, 3, 0, 1, 0, 2), (1, 2, 0, 1, 0, 2),
    (1, 0, 1, -1, 0, 0), (1, 1, 1, 0, 1, 2), (1, 3, 1, 0, 1, 2), (1, 0, 1, 0, 1, 2),
    (2, 1, 1, 0, -1, 2), (2, 2, 1, 0, -1, 2), (2, 0, 1, 0, -1, 2), (2, 3, 0, -1, 0, 2),
    (3, 1, 1, 1, 0, 1), (3, 3, 0, 0, 1, 2), (5, 2, 0, -1, 0, 2), (5, 0, 0, -1, 0, 0),
    (6, 2, 0, 1, -1, 2), (6, 1, 1, 0, 2, 2), (6, 3, 1, 0, 2, 2), (6, 0, 1, 0, 2, 2),
    (6, 0, 1, -1, 1, 0), (6, 1, 1, 1, 1, 1), (7, 1, 1, 1, -1, 1), (7, 3, 0, -1, 1, 2),
    (7, 2, 1, 0, -2, 2), (7, 0, 1, 0, -2, 2), (10, 3, 0, 0, 2, 2), (10, 1, 1, 0, -2, 2),
    (10, 2, 0, 0, -2, 2), (12, 1, 1, 1, 2, 1), (12, 2, 0, -1, -1, 2), (12, 3, 1, 0, 3, 1),
    (12, 0, 1, 0, 3, 2), (12, 2, 0, 2, 0, 2), (12, 3, 0, 2, 0, 2), (13, 1, 1, 0, -3, 2),
    (13, 0, 1, 0, -3, 2), (13, 3, 0, -1, 2, 2), (13, 3, 0, 1, 1, 2), (14, 2, 0, -1, -2, 2),
    (14, 0, 1, -1, 2, 0), (15, 1, 1, 0, 3, 2), (15, 2, 1, 0, -3, 0), (15, 0, 1, -1, -2, 0),
    (15, 3, 0, 0, 3, 1), (16, 2, 0, 0, -3, 0), (16, 1, 1, 1, -2, 1), (17, 0, 1, -1, 3, 0),
    (18, 2, 0, 2, -1, 2), (18, 1, 1, 1, -3, 1), (18, 3, 0, 2, 1, 2), (19, 0, 1, -1, -3, 0),
    (19, 2, 0, 1, -2, 2), (19, 2, 0, -1, -3, 0), (20, 3, 0, -1, 3, 1), (21, 3, 0, 1, 2, 2),
    (22, 1, 1, 0, 4, 2), (22, 0, 1, 0, 4, 2), (22, 0, 1, -1, -1, 0), (22, 1, 1, 1, 3, 1),
    (22, 2, 0, 2, -2, 2), (22, 3, 0, 2, 2, 2), (25, 3, 0, 1, 3, 1), (26, 2, 0, 1, -3, 0),
    (26, 1, 1, 1, 4, 1), (26, 0, 1, -1, 4, 0), (27, 2, 0, 2, -3, 0), (27, 3, 0, 2, 3, 1),
)

TOK, FEA, HID = 384, 256, 512
SPLIT = 160
PARTS = ((0, SPLIT), (SPLIT, TOK))
STEPS = len(ORDER)
HALF = FEA // 2
LAG = 10
GATE_LAG = 16
END_LAG = 22
MOST = max(LAG, GATE_LAG - 3)
SCALE = 256 * 5.45
CODED = HALF + HALF // 4


def landed(send):
    _, link, part, dy, dz, rows = send
    dy += (-1, 1, 0, 0)[link]
    dz += (0, 0, -1, 1)[link]
    return part, (2 if dy == -2 else dy), (4 if dz == -4 else dz), rows


def rows_of(part, rows):
    start, stop = PARTS[part]
    middle = (start + stop) // 2
    lo = middle if rows == 1 else start
    hi = middle if rows == 0 else stop
    return pl.ds(lo, hi - lo)


def needed(part, dy, dz, rows):
    return [
        n
        for n, send in enumerate(SENDS)
        if landed(send)[:3] == (part, dy, dz)
        and (rows == 2 or landed(send)[3] in (2, rows))
    ]


def tree(step, lo, hi, emit):
    if hi - lo == 1:
        emit(lo)
        return
    mid = (lo + hi) // 2
    lax.cond(
        step < mid,
        lambda: tree(step, lo, mid, emit),
        lambda: tree(step, mid, hi, emit),
    )


WORDS = tuple(
    sum((dy + 1 + 4 * (dz + 3)) << (5 * n) for n, (dy, dz) in enumerate(ORDER[w : w + 6]))
    for w in range(0, STEPS, 6)
)


def offsets(step):
    word = jnp.int32(WORDS[0])
    for n, value in enumerate(WORDS[1:], 1):
        word = jnp.where(step >= 6 * n, jnp.int32(value), word)
    bits = lax.shift_right_logical(word, 5 * lax.rem(step, 6)) & 31
    return (bits & 3) - 1, lax.shift_right_logical(bits, 2) - 3


def encode(sums, ref):
    head = sums.astype(jnp.bfloat16)
    wide = head.astype(jnp.float32)
    inverse = pl.reciprocal(jnp.where(jnp.abs(wide) > 1e-37, wide, 1.0), approx=True)
    level = jnp.floor(((sums - wide) * SCALE) * inverse + 5.5)
    q = HALF // 4
    code = (level[:q] + level[q : 2 * q] * 11.0) + (level[2 * q : 3 * q] * 121.0 + level[3 * q :] * 1331.0)
    power = jnp.floor(code * (1.0 / 256.0))
    rest = code - power * 256.0
    place = jnp.where(rest >= 128.0, -rest, rest + 128.0)
    ref[:HALF] = head
    ref[HALF:] = (place * jnp.exp2(power)).astype(jnp.bfloat16)


def decode(ref):
    wide = ref[:HALF].astype(jnp.float32)
    place = ref[HALF:].astype(jnp.float32)
    size = jnp.abs(place)
    power = jnp.floor(jnp.log2(size * 1.002)) - 7.0
    size = jnp.floor(size * jnp.exp2(-power) + 0.5)
    code = power * 256.0 + jnp.where(place < 0.0, size, size - 128.0)
    one = jnp.floor((code + 0.5) * (1.0 / 1331.0))
    code = code - one * 1331.0
    two = jnp.floor((code + 0.5) * (1.0 / 121.0))
    code = code - two * 121.0
    three = jnp.floor((code + 0.5) * (1.0 / 11.0))
    level = jnp.concatenate([code - three * 11.0, three, two, one], axis=0)
    return wide + wide * ((level - 5.0) * (1.0 / SCALE))


def kernel(
    tokens, acts, weight, cov, gate,
    held, own_t, panel, total, part_sum, coded, through, from_low, from_high,
    ag_send, ag_recv, core_send, core_recv, x_send, thr_recv, low_recv, high_recv, w_sem, a_sem,
):
    dp, ten = lax.axis_index("dp"), lax.axis_index("tensor")
    x, core = dp // 2, dp % 2
    z, y = ten // 4, ten % 4

    def at(x_, core_, y_, z_):
        return (x_ * 2 + core_, z_ * 4 + y_)

    links = (
        at(x, core, (y + 1) % 4, z),
        at(x, core, (y + 3) % 4, z),
        at(x, core, y, (z + 1) % 8),
        at(x, core, y, (z + 7) % 8),
    )
    other = at(x, 1 - core, y, z)
    x_up = at((x + 1) % 4, core, y, z)
    x_down = at((x + 3) % 4, core, y, z)

    def block(dy, dz):
        return ((z + dz + 8) % 8) * 4 + (y + dy + 4) % 4

    own = block(0, 0)
    barrier = pltpu.get_barrier_semaphore()
    for device in (*links, other, x_up, x_down):
        pl.semaphore_signal(barrier, inc=1, device_id=device, device_id_type=MESH)
    a_copy = pltpu.make_async_copy(acts, held.at[own, pl.ds(0, TOK)], a_sem)
    a_copy.start()
    w_copy = pltpu.make_async_copy(weight, panel, w_sem)
    w_copy.start()
    total[...] = jnp.zeros_like(total)
    pl.semaphore_wait(barrier, 7)

    def gather(n):
        _, link, part, dy, dz, rows = SENDS[n]
        ref = held.at[block(dy, dz), rows_of(part, rows)]
        return pltpu.make_async_remote_copy(
            src_ref=acts.at[rows_of(part, rows)] if dy == dz == 0 else ref,
            dst_ref=ref,
            send_sem=ag_send.at[n],
            recv_sem=ag_recv.at[n],
            device_id=links[link],
            device_id_type=MESH,
        )

    def arrived(n):
        part, dy, dz, rows = landed(SENDS[n])
        ref = held.at[block(dy, dz), rows_of(part, rows)]
        pltpu.make_async_remote_copy(
            src_ref=ref,
            dst_ref=ref,
            send_sem=ag_send.at[n],
            recv_sem=ag_recv.at[n],
            device_id=links[SENDS[n][1]],
            device_id_type=MESH,
        ).wait_recv()

    events = [[] for _ in range(STEPS + 1)]
    seen = set()

    def want(step, receives):
        for n in receives:
            if n not in seen:
                seen.add(n)
                events[step + 1].append((arrived, n))

    for step in range(-1, STEPS):
        for n, send in enumerate(SENDS):
            if send[0] == step:
                want(step, needed(*send[2:]))
                events[step + 1].append((lambda m: gather(m).start(), n))
        if step >= 0:
            for part in range(2):
                want(step, needed(part, *ORDER[step], 2))

    def run(step):
        for action, n in events[step + 1]:
            action(n)

    def where(step):
        dy, dz = offsets(step)
        plane, col = (z + dz + 8) & 7, (y + dy + 4) & 3
        hops = (lax.shift_right_logical(plane, 1) - x + 4) & 3
        return plane * 4 + col, col, hops, (plane & 1) == core

    def to_core(step, k):
        return pltpu.make_async_remote_copy(
            src_ref=held.at[k, pl.ds(0, TOK)],
            dst_ref=held.at[k, pl.ds(TOK, TOK)],
            send_sem=core_send.at[step],
            recv_sem=core_recv.at[step],
            device_id=other,
            device_id_type=MESH,
        )

    def along_x(step, half, dst, recv_sem, device):
        return pltpu.make_async_remote_copy(
            src_ref=coded.at[step, half],
            dst_ref=dst,
            send_sem=x_send.at[2 * step + half],
            recv_sem=recv_sem,
            device_id=device,
            device_id_type=MESH,
        )

    def thr(step, half, side, col, device):
        slot = 4 * side + col
        return along_x(step, half, through.at[slot], thr_recv.at[slot], device)

    def low(step, half, col):
        return along_x(step, half, from_low.at[2 * col + half], low_recv.at[2 * col + half], x_up)

    def high(step, half, col):
        return along_x(step, half, from_high.at[2 * col + half], high_recv.at[2 * col + half], x_down)

    def share(step):
        k, _, _, mine = where(step)

        @pl.when(jnp.logical_not(mine) | (step == 0))
        def _():
            to_core(step, k).start()

    def partial(step):
        k, col, hops, mine = where(step)

        @pl.when(mine)
        def _():
            @pl.when(step > 0)
            def _():
                to_core(step, k).wait_recv()

            part_sum[step] = jnp.dot(own_t[...], held[k], preferred_element_type=jnp.float32)

            @pl.when((hops == 2) | (hops == 3))
            def _():
                encode(part_sum[step, :HALF], coded.at[step, 0])

            @pl.when(hops == 2)
            def _():
                thr(step, 0, 0, col, x_up).start()

            @pl.when(hops == 3)
            def _():
                high(step, 0, col).start()

            @pl.when((hops == 2) | (hops == 1))
            def _():
                encode(part_sum[step, HALF:], coded.at[step, 1])

            @pl.when(hops == 2)
            def _():
                thr(step, 1, 1, col, x_down).start()

            @pl.when(hops == 1)
            def _():
                low(step, 1, col).start()

    def pass_on(step):
        _, col, hops, mine = where(step)

        @pl.when(mine & (hops == 1))
        def _():
            thr(step, 0, 0, col, x_up).wait_recv()
            encode(part_sum[step, :HALF] + decode(through.at[col]), coded.at[step, 0])
            low(step, 0, col).start()

        @pl.when(mine & (hops == 3))
        def _():
            thr(step, 1, 1, col, x_down).wait_recv()
            encode(part_sum[step, HALF:] + decode(through.at[4 + col]), coded.at[step, 1])
            high(step, 1, col).start()

    def product(step):
        k, _, _, _ = where(step)
        rows = pl.ds(pl.multiple_of(k * FEA, FEA), FEA)
        return jnp.dot(held[k, :TOK], panel[rows, :], preferred_element_type=jnp.float32)

    def project(step):
        total[...] += (product(step) + product(step + 1)) + (product(step + 2) + product(step + 3))

    def finish(step):
        _, col, hops, mine = where(step)

        @pl.when(mine & (hops == 0))
        def _():
            for half in range(2):
                low(step, half, col).wait_recv()
                high(step, half, col).wait_recv()
                slot = 2 * col + half
                rows = pl.ds(half * HALF, HALF)
                sums = part_sum[step, rows] + (decode(from_low.at[slot]) + decode(from_high.at[slot]))
                columns = pl.ds(pl.multiple_of(col * FEA, FEA), FEA)
                cov[rows, columns] = sums / jnp.float32(tokens)

    def sent(step):
        k, col, hops, mine = where(step)

        @pl.when(jnp.logical_not(mine) | (step == 0))
        def _():
            to_core(step, k).wait_send()

        @pl.when(mine & (hops != 0))
        def _():
            for half in range(2):
                low(step, half, col).wait_send()

    run(-1)
    a_copy.wait()
    share(0)
    own_t[:, :TOK] = held[own, :TOK].T
    to_core(0, own).wait_recv()
    own_t[:, TOK:] = held[own, TOK:].T
    w_copy.wait()

    def step_body(step, _):
        @pl.when(step < STEPS)
        def _():
            tree(step, 0, STEPS, run)

        @pl.when((step > 0) & (step < STEPS))
        def _():
            share(step)

        @pl.when((step >= 1) & (step < STEPS + 1))
        def _():
            partial(step - 1)

        @pl.when((step >= LAG) & (step < STEPS + LAG))
        def _():
            pass_on(step - LAG)

        @pl.when((step >= GATE_LAG) & (step % 4 == GATE_LAG % 4))
        def _():
            project(step - GATE_LAG)

        @pl.when(step >= END_LAG)
        def _():
            finish(step - END_LAG)

        return 0

    lax.fori_loop(0, STEPS + MOST, step_body, 0)
    gate[...] = total[...].astype(gate.dtype)

    def last_body(step, _):
        finish(step)
        return 0

    def sent_body(step, _):
        sent(step)
        return 0

    lax.fori_loop(0, STEPS, sent_body, 0)
    for n in range(len(SENDS)):
        gather(n).wait_send()
    lax.fori_loop(STEPS + MOST - END_LAG, STEPS, last_body, 0)


def leave(cov_in, gate_in, cov, gate, sem):
    one = pltpu.make_async_copy(cov_in, cov, sem.at[0])
    two = pltpu.make_async_copy(gate_in, gate, sem.at[1])
    one.start()
    two.start()
    one.wait()
    two.wait()


def solution(mesh):
    def step(acts, weight):
        tokens = acts.shape[0] * mesh.shape["dp"]
        sems = pltpu.SemaphoreType.DMA
        f32, bf16 = jnp.float32, jnp.bfloat16
        sums = pl.pallas_call(
            functools.partial(kernel, tokens),
            out_shape=(
                pltpu.VMEM((FEA, 4 * FEA), f32),
                pltpu.VMEM((TOK, HID), bf16),
            ),
            in_specs=[pl.BlockSpec(memory_space=pl.ANY)] * 2,
            out_specs=[pl.BlockSpec(memory_space=pltpu.VMEM)] * 2,
            scratch_shapes=[
                pltpu.VMEM((32, 2 * TOK, FEA), bf16),
                pltpu.VMEM((FEA, 2 * TOK), bf16),
                pltpu.VMEM((32 * FEA, HID), bf16),
                pltpu.VMEM((TOK, HID), f32),
                pltpu.VMEM((STEPS, FEA, FEA), f32),
                pltpu.VMEM((STEPS, 2, CODED, FEA), bf16),
                pltpu.VMEM((8, CODED, FEA), bf16),
                pltpu.VMEM((8, CODED, FEA), bf16),
                pltpu.VMEM((8, CODED, FEA), bf16),
                sems((len(SENDS),)),
                sems((len(SENDS),)),
                sems((STEPS,)),
                sems((STEPS,)),
                sems((2 * STEPS,)),
                sems((8,)),
                sems((8,)),
                sems((8,)),
                sems(()),
                sems(()),
            ],
            compiler_params=pltpu.CompilerParams(
                collective_id=0, has_side_effects=True, vmem_limit_bytes=56 * 2**20
            ),
        )(acts, weight)
        return pl.pallas_call(
            leave,
            out_shape=(
                jax.ShapeDtypeStruct((FEA, 4 * FEA), f32),
                jax.ShapeDtypeStruct((TOK, HID), bf16),
            ),
            in_specs=[pl.BlockSpec(memory_space=pltpu.VMEM)] * 2,
            out_specs=[pl.BlockSpec(memory_space=pl.ANY)] * 2,
            scratch_shapes=[sems((2,))],
            compiler_params=pltpu.CompilerParams(vmem_limit_bytes=4 * 2**20),
        )(*(pltpu.with_memory_space_constraint(s, pltpu.VMEM) for s in sums))

    return jax.shard_map(
        step,
        mesh=mesh,
        in_specs=(P("dp", "tensor"), P(None, "tensor")),
        out_specs=(P("tensor", "dp"), P("dp", "tensor")),
        check_vma=False,
    )
```

```python
import functools

import jax
import jax.numpy as jnp
from jax import lax
from jax.experimental import pallas as pl
from jax.experimental.pallas import tpu as pltpu
from jax.sharding import PartitionSpec as P

MESH = pl.DeviceIdType.MESH

ORDER = (
    (0, 0), (-1, 0), (0, -1), (0, 1), (1, 0), (1, 1), (1, -1), (-1, 1),
    (0, -2), (0, 2), (2, 0), (-1, -1), (-1, 2), (0, 3), (-1, -2), (0, -3),
    (1, -2), (-1, 3), (2, 1), (-1, -3), (1, 2), (0, 4), (2, -2), (2, 2),
    (1, 3), (1, -3), (-1, 4), (2, -3), (2, 3), (2, -1), (1, 4), (2, 4),
)

SENDS = (
    (-1, 0, 1, 0, 0, 2), (-1, 1, 0, 0, 0, 2), (-1, 2, 0, 0, 0, 2), (-1, 3, 1, 0, 0, 2),
    (-1, 1, 1, 0, 0, 2), (-1, 2, 1, 0, 0, 2), (-1, 0, 0, 0, 0, 2), (-1, 3, 0, 0, 0, 2),
    (1, 1, 0, 1, 0, 1), (1, 2, 0, 0, -1, 2), (1, 3, 0, 1, 0, 2), (1, 2, 0, 1, 0, 2),
    (1, 0, 1, -1, 0, 0), (1, 1, 1, 0, 1, 2), (1, 3, 1, 0, 1, 2), (1, 0, 1, 0, 1, 2),
    (2, 1, 1, 0, -1, 2), (2, 2, 1, 0, -1, 2), (2, 0, 1, 0, -1, 2), (2, 3, 0, -1, 0, 2),
    (3, 1, 1, 1, 0, 1), (3, 3, 0, 0, 1, 2), (5, 2, 0, -1, 0, 2), (5, 0, 0, -1, 0, 0),
    (6, 2, 0, 1, -1, 2), (6, 1, 1, 0, 2, 2), (6, 3, 1, 0, 2, 2), (6, 0, 1, 0, 2, 2),
    (6, 0, 1, -1, 1, 0), (6, 1, 1, 1, 1, 1), (7, 1, 1, 1, -1, 1), (7, 3, 0, -1, 1, 2),
    (7, 2, 1, 0, -2, 2), (7, 0, 1, 0, -2, 2), (10, 3, 0, 0, 2, 2), (10, 1, 1, 0, -2, 2),
    (10, 2, 0, 0, -2, 2), (12, 1, 1, 1, 2, 1), (12, 2, 0, -1, -1, 2), (12, 3, 1, 0, 3, 1),
    (12, 0, 1, 0, 3, 2), (12, 2, 0, 2, 0, 2), (12, 3, 0, 2, 0, 2), (13, 1, 1, 0, -3, 2),
    (13, 0, 1, 0, -3, 2), (13, 3, 0, -1, 2, 2), (13, 3, 0, 1, 1, 2), (14, 2, 0, -1, -2, 2),
    (14, 0, 1, -1, 2, 0), (15, 1, 1, 0, 3, 2), (15, 2, 1, 0, -3, 0), (15, 0, 1, -1, -2, 0),
    (15, 3, 0, 0, 3, 1), (16, 2, 0, 0, -3, 0), (16, 1, 1, 1, -2, 1), (17, 0, 1, -1, 3, 0),
    (18, 2, 0, 2, -1, 2), (18, 1, 1, 1, -3, 1), (18, 3, 0, 2, 1, 2), (19, 0, 1, -1, -3, 0),
    (19, 2, 0, 1, -2, 2), (19, 2, 0, -1, -3, 0), (20, 3, 0, -1, 3, 1), (21, 3, 0, 1, 2, 2),
    (22, 1, 1, 0, 4, 2), (22, 0, 1, 0, 4, 2), (22, 0, 1, -1, -1, 0), (22, 1, 1, 1, 3, 1),
    (22, 2, 0, 2, -2, 2), (22, 3, 0, 2, 2, 2), (25, 3, 0, 1, 3, 1), (26, 2, 0, 1, -3, 0),
    (26, 1, 1, 1, 4, 1), (26, 0, 1, -1, 4, 0), (27, 2, 0, 2, -3, 0), (27, 3, 0, 2, 3, 1),
)

TOK, FEA, HID = 384, 256, 512
SPLIT = 160
PARTS = ((0, SPLIT), (SPLIT, TOK))
STEPS = len(ORDER)
HALF = FEA // 2
LAG = 10
GATE_LAG = 16
SENT_LAG = 24
END_LAG = 22
MOST = max(LAG, GATE_LAG - 3)
SCALE = 256 * 5.45
CODED = HALF + HALF // 4


def landed(send):
    _, link, part, dy, dz, rows = send
    dy += (-1, 1, 0, 0)[link]
    dz += (0, 0, -1, 1)[link]
    return part, (2 if dy == -2 else dy), (4 if dz == -4 else dz), rows


def rows_of(part, rows):
    start, stop = PARTS[part]
    middle = (start + stop) // 2
    lo = middle if rows == 1 else start
    hi = middle if rows == 0 else stop
    return pl.ds(lo, hi - lo)


def needed(part, dy, dz, rows):
    return [
        n
        for n, send in enumerate(SENDS)
        if landed(send)[:3] == (part, dy, dz)
        and (rows == 2 or landed(send)[3] in (2, rows))
    ]


def tree(step, lo, hi, emit):
    if hi - lo == 1:
        emit(lo)
        return
    mid = (lo + hi) // 2
    lax.cond(
        step < mid,
        lambda: tree(step, lo, mid, emit),
        lambda: tree(step, mid, hi, emit),
    )


WORDS = tuple(
    sum((dy + 1 + 4 * (dz + 3)) << (5 * n) for n, (dy, dz) in enumerate(ORDER[w : w + 6]))
    for w in range(0, STEPS, 6)
)


def offsets(step):
    word = jnp.int32(WORDS[0])
    for n, value in enumerate(WORDS[1:], 1):
        word = jnp.where(step >= 6 * n, jnp.int32(value), word)
    bits = lax.shift_right_logical(word, 5 * lax.rem(step, 6)) & 31
    return (bits & 3) - 1, lax.shift_right_logical(bits, 2) - 3


def encode(sums, ref):
    head = sums.astype(jnp.bfloat16)
    wide = head.astype(jnp.float32)
    inverse = pl.reciprocal(jnp.where(jnp.abs(wide) > 1e-37, wide, 1.0), approx=True)
    level = jnp.floor(((sums - wide) * SCALE) * inverse + 5.5)
    q = HALF // 4
    code = (level[:q] + level[q : 2 * q] * 11.0) + (level[2 * q : 3 * q] * 121.0 + level[3 * q :] * 1331.0)
    power = jnp.floor(code * (1.0 / 256.0))
    rest = code - power * 256.0
    place = jnp.where(rest >= 128.0, -rest, rest + 128.0)
    ref[:HALF] = head
    ref[HALF:] = (place * jnp.exp2(power)).astype(jnp.bfloat16)


def decode(ref):
    wide = ref[:HALF].astype(jnp.float32)
    place = ref[HALF:].astype(jnp.float32)
    size = jnp.abs(place)
    power = jnp.floor(jnp.log2(size * 1.002)) - 7.0
    size = jnp.floor(size * jnp.exp2(-power) + 0.5)
    code = power * 256.0 + jnp.where(place < 0.0, size, size - 128.0)
    one = jnp.floor((code + 0.5) * (1.0 / 1331.0))
    code = code - one * 1331.0
    two = jnp.floor((code + 0.5) * (1.0 / 121.0))
    code = code - two * 121.0
    three = jnp.floor((code + 0.5) * (1.0 / 11.0))
    level = jnp.concatenate([code - three * 11.0, three, two, one], axis=0)
    return wide + wide * ((level - 5.0) * (1.0 / SCALE))


def kernel(
    tokens, acts, weight, cov, gate,
    held, own_t, panel, total, part_sum, coded, through, from_low, from_high,
    ag_send, ag_recv, core_send, core_recv, x_send, thr_recv, low_recv, high_recv, w_sem, a_sem,
):
    dp, ten = lax.axis_index("dp"), lax.axis_index("tensor")
    x, core = dp // 2, dp % 2
    z, y = ten // 4, ten % 4

    def at(x_, core_, y_, z_):
        return (x_ * 2 + core_, z_ * 4 + y_)

    links = (
        at(x, core, (y + 1) % 4, z),
        at(x, core, (y + 3) % 4, z),
        at(x, core, y, (z + 1) % 8),
        at(x, core, y, (z + 7) % 8),
    )
    other = at(x, 1 - core, y, z)
    x_up = at((x + 1) % 4, core, y, z)
    x_down = at((x + 3) % 4, core, y, z)

    def block(dy, dz):
        return ((z + dz + 8) % 8) * 4 + (y + dy + 4) % 4

    own = block(0, 0)
    barrier = pltpu.get_barrier_semaphore()
    for device in (*links, other, x_up, x_down):
        pl.semaphore_signal(barrier, inc=1, device_id=device, device_id_type=MESH)
    a_copy = pltpu.make_async_copy(acts, held.at[own, pl.ds(0, TOK)], a_sem)
    a_copy.start()
    w_copy = pltpu.make_async_copy(weight, panel, w_sem)
    w_copy.start()
    total[...] = jnp.zeros_like(total)
    pl.semaphore_wait(barrier, 7)

    def gather(n):
        _, link, part, dy, dz, rows = SENDS[n]
        ref = held.at[block(dy, dz), rows_of(part, rows)]
        return pltpu.make_async_remote_copy(
            src_ref=acts.at[rows_of(part, rows)] if dy == dz == 0 else ref,
            dst_ref=ref,
            send_sem=ag_send.at[n],
            recv_sem=ag_recv.at[n],
            device_id=links[link],
            device_id_type=MESH,
        )

    def arrived(n):
        part, dy, dz, rows = landed(SENDS[n])
        ref = held.at[block(dy, dz), rows_of(part, rows)]
        pltpu.make_async_remote_copy(
            src_ref=ref,
            dst_ref=ref,
            send_sem=ag_send.at[n],
            recv_sem=ag_recv.at[n],
            device_id=links[SENDS[n][1]],
            device_id_type=MESH,
        ).wait_recv()

    events = [[] for _ in range(STEPS + 1)]
    seen = set()

    def want(step, receives):
        for n in receives:
            if n not in seen:
                seen.add(n)
                events[step + 1].append((arrived, n))

    for step in range(-1, STEPS):
        for n, send in enumerate(SENDS):
            if send[0] == step:
                want(step, needed(*send[2:]))
                events[step + 1].append((lambda m: gather(m).start(), n))
        if step >= 0:
            for part in range(2):
                want(step, needed(part, *ORDER[step], 2))
            for n, send in enumerate(SENDS):
                if send[0] == step - 9:
                    events[step + 1].append((lambda m: gather(m).wait_send(), n))
    late = [n for n, send in enumerate(SENDS) if send[0] + 9 >= STEPS]

    def run(step):
        for action, n in events[step + 1]:
            action(n)

    def where(step):
        dy, dz = offsets(step)
        plane, col = (z + dz + 8) & 7, (y + dy + 4) & 3
        hops = (lax.shift_right_logical(plane, 1) - x + 4) & 3
        return plane * 4 + col, col, hops, (plane & 1) == core

    def to_core(step, k):
        return pltpu.make_async_remote_copy(
            src_ref=held.at[k, pl.ds(0, TOK)],
            dst_ref=held.at[k, pl.ds(TOK, TOK)],
            send_sem=core_send.at[step],
            recv_sem=core_recv.at[step],
            device_id=other,
            device_id_type=MESH,
        )

    def along_x(step, half, dst, recv_sem, device):
        return pltpu.make_async_remote_copy(
            src_ref=coded.at[step, half],
            dst_ref=dst,
            send_sem=x_send.at[2 * step + half],
            recv_sem=recv_sem,
            device_id=device,
            device_id_type=MESH,
        )

    def thr(step, half, side, col, device):
        slot = 4 * side + col
        return along_x(step, half, through.at[slot], thr_recv.at[slot], device)

    def low(step, half, col):
        return along_x(step, half, from_low.at[2 * col + half], low_recv.at[2 * col + half], x_up)

    def high(step, half, col):
        return along_x(step, half, from_high.at[2 * col + half], high_recv.at[2 * col + half], x_down)

    def share(step):
        k, _, _, mine = where(step)

        @pl.when(jnp.logical_not(mine) | (step == 0))
        def _():
            to_core(step, k).start()

    def partial(step):
        k, col, hops, mine = where(step)

        @pl.when(mine)
        def _():
            @pl.when(step > 0)
            def _():
                to_core(step, k).wait_recv()

            part_sum[step] = jnp.dot(own_t[...], held[k], preferred_element_type=jnp.float32)

            @pl.when((hops == 2) | (hops == 3))
            def _():
                encode(part_sum[step, :HALF], coded.at[step, 0])

            @pl.when(hops == 2)
            def _():
                thr(step, 0, 0, col, x_up).start()

            @pl.when(hops == 3)
            def _():
                high(step, 0, col).start()

            @pl.when((hops == 2) | (hops == 1))
            def _():
                encode(part_sum[step, HALF:], coded.at[step, 1])

            @pl.when(hops == 2)
            def _():
                thr(step, 1, 1, col, x_down).start()

            @pl.when(hops == 1)
            def _():
                low(step, 1, col).start()

    def pass_on(step):
        _, col, hops, mine = where(step)

        @pl.when(mine & (hops == 1))
        def _():
            thr(step, 0, 0, col, x_up).wait_recv()
            encode(part_sum[step, :HALF] + decode(through.at[col]), coded.at[step, 0])
            low(step, 0, col).start()

        @pl.when(mine & (hops == 3))
        def _():
            thr(step, 1, 1, col, x_down).wait_recv()
            encode(part_sum[step, HALF:] + decode(through.at[4 + col]), coded.at[step, 1])
            high(step, 1, col).start()

    def product(step):
        k, _, _, _ = where(step)
        rows = pl.ds(pl.multiple_of(k * FEA, FEA), FEA)
        return jnp.dot(held[k, :TOK], panel[rows, :], preferred_element_type=jnp.float32)

    def project(step):
        total[...] += (product(step) + product(step + 1)) + (product(step + 2) + product(step + 3))

    def finish(step):
        _, col, hops, mine = where(step)

        @pl.when(mine & (hops == 0))
        def _():
            for half in range(2):
                low(step, half, col).wait_recv()
                high(step, half, col).wait_recv()
                slot = 2 * col + half
                rows = pl.ds(half * HALF, HALF)
                sums = part_sum[step, rows] + (decode(from_low.at[slot]) + decode(from_high.at[slot]))
                columns = pl.ds(pl.multiple_of(col * FEA, FEA), FEA)
                cov[rows, columns] = sums * jnp.float32(1.0 / tokens)

    def sent(step):
        k, col, hops, mine = where(step)

        @pl.when(jnp.logical_not(mine) | (step == 0))
        def _():
            to_core(step, k).wait_send()

        @pl.when(mine & (hops != 0))
        def _():
            for half in range(2):
                low(step, half, col).wait_send()

    run(-1)
    a_copy.wait()
    share(0)
    own_t[:, :TOK] = held[own, :TOK].T
    to_core(0, own).wait_recv()
    own_t[:, TOK:] = held[own, TOK:].T

    def step_body(step, _):
        @pl.when(step < STEPS)
        def _():
            tree(step, 0, STEPS, run)

        @pl.when((step > 0) & (step < STEPS))
        def _():
            share(step)

        @pl.when((step >= 1) & (step < STEPS + 1))
        def _():
            partial(step - 1)

        @pl.when((step >= LAG) & (step < STEPS + LAG))
        def _():
            pass_on(step - LAG)

        @pl.when((step >= GATE_LAG) & (step % 4 == GATE_LAG % 4))
        def _():
            @pl.when(step == GATE_LAG)
            def _():
                w_copy.wait()

            project(step - GATE_LAG)

        @pl.when(step >= END_LAG)
        def _():
            finish(step - END_LAG)

        @pl.when(step >= SENT_LAG)
        def _():
            sent(step - SENT_LAG)

        return 0

    lax.fori_loop(0, STEPS + MOST, step_body, 0)
    gate[...] = total[...].astype(gate.dtype)

    def last_body(step, _):
        finish(step)
        return 0

    def sent_body(step, _):
        sent(step)
        return 0

    lax.fori_loop(STEPS + MOST - SENT_LAG, STEPS, sent_body, 0)
    for n in late:
        gather(n).wait_send()
    lax.fori_loop(STEPS + MOST - END_LAG, STEPS, last_body, 0)


def leave(cov_in, gate_in, cov, gate, sem):
    one = pltpu.make_async_copy(cov_in, cov, sem.at[0])
    two = pltpu.make_async_copy(gate_in, gate, sem.at[1])
    one.start()
    two.start()
    one.wait()
    two.wait()


def solution(mesh):
    def step(acts, weight):
        tokens = acts.shape[0] * mesh.shape["dp"]
        sems = pltpu.SemaphoreType.DMA
        f32, bf16 = jnp.float32, jnp.bfloat16
        sums = pl.pallas_call(
            functools.partial(kernel, tokens),
            out_shape=(
                pltpu.VMEM((FEA, 4 * FEA), f32),
                pltpu.VMEM((TOK, HID), bf16),
            ),
            in_specs=[pl.BlockSpec(memory_space=pl.ANY)] * 2,
            out_specs=[pl.BlockSpec(memory_space=pltpu.VMEM)] * 2,
            scratch_shapes=[
                pltpu.VMEM((32, 2 * TOK, FEA), bf16),
                pltpu.VMEM((FEA, 2 * TOK), bf16),
                pltpu.VMEM((32 * FEA, HID), bf16),
                pltpu.VMEM((TOK, HID), f32),
                pltpu.VMEM((STEPS, FEA, FEA), f32),
                pltpu.VMEM((STEPS, 2, CODED, FEA), bf16),
                pltpu.VMEM((8, CODED, FEA), bf16),
                pltpu.VMEM((8, CODED, FEA), bf16),
                pltpu.VMEM((8, CODED, FEA), bf16),
                sems((len(SENDS),)),
                sems((len(SENDS),)),
                sems((STEPS,)),
                sems((STEPS,)),
                sems((2 * STEPS,)),
                sems((8,)),
                sems((8,)),
                sems((8,)),
                sems(()),
                sems(()),
            ],
            compiler_params=pltpu.CompilerParams(
                collective_id=0, has_side_effects=True, vmem_limit_bytes=56 * 2**20
            ),
        )(acts, weight)
        return pl.pallas_call(
            leave,
            out_shape=(
                jax.ShapeDtypeStruct((FEA, 4 * FEA), f32),
                jax.ShapeDtypeStruct((TOK, HID), bf16),
            ),
            in_specs=[pl.BlockSpec(memory_space=pltpu.VMEM)] * 2,
            out_specs=[pl.BlockSpec(memory_space=pl.ANY)] * 2,
            scratch_shapes=[sems((2,))],
            compiler_params=pltpu.CompilerParams(vmem_limit_bytes=4 * 2**20),
        )(*(pltpu.with_memory_space_constraint(s, pltpu.VMEM) for s in sums))

    return jax.shard_map(
        step,
        mesh=mesh,
        in_specs=(P("dp", "tensor"), P(None, "tensor")),
        out_specs=(P("tensor", "dp"), P("dp", "tensor")),
        check_vma=False,
    )
```
